1024 devices in a mesh: rep: 8 (over z_lo), node: 16 (over y, core), local: 8 (over x, z_hi).
Axes of the slice: x: 4, y: 8, z: 16 (z_hi: 2, z_lo: 8; z = z_hi * 8 + z_lo), core: 2. Of those that a mesh axis runs over, the one named last changes fastest.
Arguments:
- activations: bfloat16 [16384, 3584], P(('rep', 'node', 'local')), may hold values from -6 to 6
- cotangent: bfloat16 [16384, 1024], P(('rep', 'node', 'local')), may hold values from -6 to 6
- gates: bfloat16 [16384, 8], P(('rep', 'node', 'local')), may hold values from 0.049804688 to 0.5
- experts: int32 [16384, 8], P(('rep', 'node', 'local')), may hold values from 0 to 7, as said below
- groups: int32 [16384, 4], P(('rep', 'node', 'local')), may hold values from 0 to 15, as said below
- weights: bfloat16 [128, 3584, 1024], P(('node', 'local')), may hold values from -0.09375 to 0.09375
Outputs:
- output: bfloat16 [16384, 1024], P(('rep', 'node', 'local'))
- grad_activations: bfloat16 [16384, 3584], P(('rep', 'node', 'local'))
- grad_gates: bfloat16 [16384, 8], P(('rep', 'node', 'local'))
- grad_weights: float32 [128, 3584, 1024], P(('node', 'local'), 'rep')
The draws below stay inside these ranges and needn't reach their ends.
Inputs may be any that keep to these rules, and one draw needn't show every extreme that they name: Each token names 4 different groups. The tokens of one device fall into aligned blocks of 4 consecutive tokens, and in every block each group is named by exactly one token. experts[n, 2k] and experts[n, 2k + 1] differ. Consider the rows that reach the device of local index l in group g: one for every token, on a device of local index l of the same replica, that names g, taken in the order of the source group g2 and then of the token's block b (place g2 * 4 + b). At most 21 of these 64 rows name any one expert of group g, and for every such device one expert is named by exactly 21 of them.
All inputs are finite; a program needn't handle non-finite values.
Results may differ from the reference program's by a relative error of at most 0.013.
Values may be sent and summed in bfloat16 or wider, within the bound.
No kernel may reach another device: no remote copies, remote signals or barrier semaphores. Data moves between devices by JAX's collectives and lax.ppermute only.
A program may use at most 64 MiB of HBM per device.

```python
import math
import jax
import jax.numpy as jnp
from jax import lax

D = 3584
H = 1024
TOPK = 8
GROUPS_TOP = 4
PER_GROUP = 2
TOK_DEV = 16
EXPERTS = 128
TOKENS = 16384
CAP_N = 4
ROWS2 = 64
CAP_L = 21
N_REP = 8
N_NODE = 16
N_LOCAL = 8


def routing(key):
    per_block = N_NODE // GROUPS_TOP
    block_total = TOK_DEV // per_block
    device_total = N_REP * N_NODE * N_LOCAL
    key_groups = jax.random.fold_in(key, 101)
    key_labels = jax.random.fold_in(key, 102)
    key_rows = jax.random.fold_in(key, 103)
    group_score = jax.random.randint(key_groups, (device_total, block_total, N_NODE), 0, 1 << 20) * N_NODE + jnp.arange(N_NODE, dtype=jnp.int32)
    chosen = jnp.argsort(group_score, axis=-1).astype(jnp.int32).reshape(device_total, TOK_DEV, GROUPS_TOP)
    label_score = jax.random.randint(key_labels, (device_total, N_LOCAL), 0, 1 << 20) * N_LOCAL + jnp.arange(N_LOCAL, dtype=jnp.int32)
    label_order = jnp.argsort(label_score, axis=-1).astype(jnp.int32)
    row_score = jax.random.randint(key_rows, (device_total, ROWS2), 0, 1 << 20) * ROWS2 + jnp.arange(ROWS2, dtype=jnp.int32)
    row_order = jnp.argsort(row_score, axis=-1).astype(jnp.int32)
    positions = jnp.arange(2 * ROWS2, dtype=jnp.int32)
    others = max(N_LOCAL - 1, 1)
    which = jnp.where(positions < CAP_L, 0, 1 + (positions - CAP_L) % others).astype(jnp.int32)
    labels = label_order[:, which]
    first_local = jnp.take_along_axis(labels, row_order, axis=1)
    second_local = jnp.take_along_axis(labels, row_order + ROWS2, axis=1)
    device = jnp.arange(device_total, dtype=jnp.int32)
    rep_index = device // (N_NODE * N_LOCAL)
    node_index = device // N_LOCAL % N_NODE
    local_index = device % N_LOCAL
    receiver = (rep_index[:, None, None] * N_NODE + chosen) * N_LOCAL + local_index[:, None, None]
    slot = node_index[:, None, None] * CAP_N + (jnp.arange(TOK_DEV, dtype=jnp.int32) // per_block)[None, :, None]
    first_expert = first_local[receiver, slot]
    second_expert = second_local[receiver, slot]
    expert_ids = jnp.stack([first_expert, second_expert], axis=-1).reshape(TOKENS, TOPK)
    return (chosen.reshape(TOKENS, GROUPS_TOP), expert_ids.astype(jnp.int32))


def draw_experts(key, part):
    chosen, expert_ids = routing(key)
    return expert_ids


def draw_groups(key, part):
    chosen, expert_ids = routing(key)
    return chosen


def shard_levels(rng, shape, pieces, smallest, largest):
    level, own = 1.0, jax.random.fold_in(rng, 6)
    for axis_at, parts in pieces:
        steps = jnp.exp(jax.random.uniform(jax.random.fold_in(own, axis_at), (parts,), jnp.float32, smallest / len(pieces), largest / len(pieces)))
        level = level * jnp.repeat(steps, shape[axis_at] // parts).reshape([-1 if axis == axis_at else 1 for axis in range(len(shape))])
    return level


def noise(stream_key, extent, scale, bound, shards=(), held_as=jnp.bfloat16):
    factor_of = shard_levels(stream_key, extent, shards, -0.22, 0.18) if shards else 1.0
    values = jax.random.normal(stream_key, extent, jnp.float32) * scale * factor_of
    return jnp.minimum(jnp.maximum(values, -bound), bound).astype(held_as)


def setup_inputs(seed: int = 0) -> dict:
    arg_keys = jax.random.split(jax.random.key(seed), 7)
    activations = noise(arg_keys[0], (TOKENS, D), 1.0, 6.0, ((0, 1024),))
    cotangent = noise(arg_keys[1], (TOKENS, H), 1.0, 6.0, ((0, 1024),))
    gates = jnp.clip(jnp.exp(math.log(0.5) - 2.306499 * jax.random.uniform(arg_keys[2], (TOKENS, TOPK), jnp.float32) ** shard_levels(arg_keys[2], (TOKENS, TOPK), ((0, 1024),), -0.2, 0.2)), 0.049804688, 0.5).astype(jnp.bfloat16)
    experts = draw_experts(jax.random.fold_in(arg_keys[6], 71), 0)
    groups = draw_groups(jax.random.fold_in(arg_keys[6], 71), 0)
    weights = noise(arg_keys[5], (EXPERTS, D, H), D ** -0.5, 0.09375, ((0, 128),))
    return dict(activations=activations, cotangent=cotangent, gates=gates, experts=experts, groups=groups, weights=weights)


def reference(activations, cotangent, gates, experts, groups, weights):
    pair_total = TOKENS * TOPK
    slot_cap = N_REP * N_LOCAL * CAP_L
    group_slots = jnp.repeat(groups.astype(jnp.int32), PER_GROUP, axis=1)
    expert_full = group_slots * N_LOCAL + experts.astype(jnp.int32)
    expert_flat = expert_full.reshape(pair_total).astype(jnp.int32)
    hits = (expert_flat[:, None] == jnp.arange(EXPERTS, dtype=jnp.int32)[None, :]).astype(jnp.int32)
    ranks = jnp.cumsum(hits, axis=0) - 1
    my_rank = jnp.sum(ranks * hits, axis=1).astype(jnp.int32)
    pair_index = jnp.arange(pair_total, dtype=jnp.int32)
    table = jnp.full((EXPERTS, slot_cap), pair_total, jnp.int32).at[expert_flat, my_rank].set(pair_index)
    token_table = jnp.where(table < pair_total, table // TOPK, TOKENS).astype(jnp.int32)
    gate_pad = jnp.concatenate([gates.reshape(pair_total), jnp.zeros((1,), gates.dtype)])
    gate_table = gate_pad[table]
    act_pad = jnp.concatenate([activations, jnp.zeros((1, D), activations.dtype)], axis=0)
    cot_pad = jnp.concatenate([cotangent, jnp.zeros((1, H), cotangent.dtype)], axis=0)

    def per_expert(bundle):
        expert_weight, rows_index, row_gates = bundle
        rows_in = act_pad[rows_index]
        rows_cot = cot_pad[rows_index]
        pre_act = jnp.dot(rows_in, expert_weight, preferred_element_type=jnp.float32)
        sigmoid_pre = jax.nn.sigmoid(pre_act)
        activated = (pre_act * sigmoid_pre).astype(jnp.bfloat16)
        slope_term = sigmoid_pre * (1.0 + pre_act * (1.0 - sigmoid_pre))
        grad_pre = (row_gates.astype(jnp.float32)[:, None] * rows_cot.astype(jnp.float32) * slope_term).astype(jnp.bfloat16)
        grad_rows = jnp.dot(grad_pre, expert_weight.T, preferred_element_type=jnp.float32).astype(jnp.bfloat16)
        grad_weight = jnp.dot(rows_in.T, grad_pre, preferred_element_type=jnp.float32)
        return activated, grad_rows, grad_weight

    act_table, grad_table, grad_weights = lax.map(per_expert, (weights, token_table, gate_table))
    act_pairs = act_table[expert_flat, my_rank].reshape(TOKENS, GROUPS_TOP, PER_GROUP, H)
    grad_pairs = grad_table[expert_flat, my_rank].reshape(TOKENS, GROUPS_TOP, PER_GROUP, D)
    gate_pairs = gates.astype(jnp.float32).reshape(TOKENS, GROUPS_TOP, PER_GROUP)
    group_out = jnp.sum(gate_pairs[..., None] * act_pairs.astype(jnp.float32), axis=2).astype(jnp.bfloat16)
    group_grad = jnp.sum(grad_pairs.astype(jnp.float32), axis=2).astype(jnp.bfloat16)
    output = jnp.sum(group_out.astype(jnp.float32), axis=1).astype(jnp.bfloat16)
    grad_activations = jnp.sum(group_grad.astype(jnp.float32), axis=1).astype(jnp.bfloat16)
    grad_gates = jnp.einsum("nh,njh->nj", cotangent.astype(jnp.float32), act_pairs.reshape(TOKENS, TOPK, H).astype(jnp.float32)).astype(jnp.bfloat16)
    return output, grad_activations, grad_gates, grad_weights
```

```python
import jax
import jax.numpy as jnp
from jax import lax
from jax.sharding import Mesh, PartitionSpec as P

ALL = ("rep", "node", "x", "half")


def partner_pairs(reps):
    ring = 2 * reps
    step = reps // 2
    pairs = []
    for z in range(ring):
        other = z + step if (z // step) % 2 == 1 else z - step
        other %= ring
        pairs.append(((z % reps) * 2 + z // reps, (other % reps) * 2 + other // reps))
    return pairs


def on_device(activations, cotangent, gates, experts, groups, weights):
    reps = lax.axis_size("rep")
    nodes = lax.axis_size("node")
    xs = lax.axis_size("x")
    locals_ = xs * lax.axis_size("half")
    tokens, width = activations.shape
    hidden = weights.shape[2]
    slots = experts.shape[1]
    named = groups.shape[1]
    per_group = slots // named
    block = nodes // named
    blocks = tokens // block
    rows_one = nodes * blocks
    cap = max(rows_one // 3, (per_group * rows_one + locals_ - 1) // locals_)
    total = nodes * locals_
    bf = jnp.bfloat16
    f32 = jnp.float32
    pairs = partner_pairs(reps)
    rep_at = lax.axis_index("rep")
    node_at = lax.axis_index("node")
    x_at = lax.axis_index("x")
    half_at = lax.axis_index("half")

    expert_full = jnp.repeat(groups, per_group, axis=1) * locals_ + experts
    gate_wide = jnp.sum(
        jnp.where(
            expert_full[:, :, None] == jnp.arange(total, dtype=jnp.int32)[None, None, :],
            gates.astype(f32)[:, :, None],
            0.0,
        ),
        axis=1,
    ).astype(bf)
    own = jnp.concatenate([activations, cotangent, gate_wide], axis=1)
    wide = own.shape[1]
    other = lax.ppermute(own, ("rep", "half"), pairs)
    both = jnp.concatenate([own, other], axis=0)

    places = 2 * rows_one
    place_index = jnp.arange(places, dtype=jnp.int32)
    place_expert = (
        (place_index // (2 * blocks))[:, None]
        == (jnp.arange(total, dtype=jnp.int32) // locals_)[None, :]
    ).astype(bf)
    named_both = (both[:, width + hidden :] != 0).astype(bf)
    hit = lax.dot_general(
        place_expert, named_both, (((1,), (1,)), ((), ())), preferred_element_type=f32
    )
    placing = (
        (hit > 0)
        & (
            (place_index % (2 * blocks))[:, None]
            == (jnp.arange(2 * tokens, dtype=jnp.int32) // block)[None, :]
        )
    ).astype(bf)
    send_rows = jnp.dot(placing, both, preferred_element_type=f32).astype(bf)
    rows = lax.all_to_all(
        send_rows.reshape(nodes, 2 * blocks, wide), "node", 0, 0, tiled=True
    ).reshape(places, wide)

    cap2 = 2 * cap
    taken = xs * cap2
    slot_index = jnp.arange(taken, dtype=jnp.int32)
    slot_expert = (
        (node_at * locals_ + (slot_index // cap2) * 2 + half_at)[:, None]
        == jnp.arange(total, dtype=jnp.int32)[None, :]
    ).astype(bf)
    named_rows = (rows[:, width + hidden :] != 0).astype(bf)
    live = lax.dot_general(
        slot_expert, named_rows, (((1,), (1,)), ((), ())), preferred_element_type=f32
    )
    before = (place_index[:, None] < place_index[None, :]).astype(bf)
    rank = jnp.dot(live.astype(bf), before, preferred_element_type=f32)
    picker = (
        (live > 0) & (rank == (slot_index % cap2).astype(f32)[:, None])
    ).astype(bf)
    send_slots = jnp.dot(picker, rows, preferred_element_type=f32).astype(bf)
    inside = lax.all_to_all(
        send_slots.reshape(xs, cap2, wide), "x", 0, 0, tiled=True
    ).reshape(taken, wide)

    exp_x = inside[:, :width]
    exp_dy = inside[:, width : width + hidden].astype(f32)
    mine = jnp.arange(total, dtype=jnp.int32) == node_at * locals_ + x_at * 2 + half_at
    gate = jnp.sum(
        jnp.where(mine[None, :], inside[:, width + hidden :].astype(f32), 0.0), axis=1, keepdims=True
    )
    weight = weights[0]
    pre = jnp.dot(exp_x, weight, preferred_element_type=f32)
    sig = jax.nn.sigmoid(pre)
    act = (pre * sig).astype(bf).astype(f32)
    slope = sig * (1.0 + pre * (1.0 - sig))
    grad_pre = (gate * exp_dy * slope).astype(bf)
    grad_in = lax.dot_general(
        grad_pre, weight, (((1,), (1,)), ((), ())), preferred_element_type=f32
    ).astype(bf)
    grad_gate = jnp.sum(exp_dy * act, axis=1, keepdims=True)
    back = jnp.concatenate(
        [
            grad_in,
            (gate * act).astype(bf),
            jnp.where(mine[None, :], grad_gate, 0.0).astype(bf),
        ],
        axis=1,
    )

    share = width // reps
    gathered = lax.all_gather(grad_pre, "rep", axis=0, tiled=True)
    x_cols = jnp.zeros((reps * taken, share), bf)
    for k in range(reps):
        piece = lax.dynamic_slice_in_dim(exp_x, (rep_at + k) % reps * share, share, 1)
        if k:
            piece = lax.ppermute(piece, "rep", [(i, (i + k) % reps) for i in range(reps)])
        x_cols = lax.dynamic_update_slice_in_dim(
            x_cols, piece, (rep_at + reps - k) % reps * taken, 0
        )
    grad_share = lax.dot_general(
        x_cols, gathered, (((0,), (0,)), ((), ())), preferred_element_type=f32
    )

    back_slots = lax.all_to_all(
        back.reshape(xs, cap2, wide), "x", 0, 0, tiled=True
    ).reshape(taken, wide)
    back_rows = lax.dot_general(
        picker, back_slots, (((0,), (0,)), ((), ())), preferred_element_type=f32
    ).astype(bf)
    home_rows = lax.all_to_all(
        back_rows.reshape(nodes, 2 * blocks, wide), "node", 0, 0, tiled=True
    ).reshape(places, wide)
    home = lax.dot_general(
        placing, home_rows, (((0,), (0,)), ((), ())), preferred_element_type=f32
    )
    returned = lax.ppermute(home[tokens:].astype(bf), ("rep", "half"), pairs)
    result = home[:tokens] + returned.astype(f32)
    grad_activations = result[:, :width].astype(bf)
    output = result[:, width : width + hidden].astype(bf)
    gate_back = result[:, width + hidden :]
    grad_gates = jnp.sum(
        jnp.where(
            expert_full[:, :, None] == jnp.arange(total, dtype=jnp.int32)[None, None, :],
            gate_back[:, None, :],
            0.0,
        ),
        axis=2,
    ).astype(bf)
    return (output, grad_activations, grad_gates, grad_share[None])


def solution(mesh):
    reps, nodes, locals_ = (mesh.shape[name] for name in ("rep", "node", "local"))
    fine = Mesh(mesh.devices.reshape(reps, nodes, locals_ // 2, 2), ALL)
    rows = P(ALL, None)
    return jax.shard_map(
        on_device,
        mesh=fine,
        in_specs=(rows, rows, rows, rows, rows, P(("node", "x", "half"), None, None)),
        out_specs=(rows, rows, rows, P(("node", "x", "half"), "rep", None)),
        check_vma=False,
    )
```

```python
import jax
import jax.numpy as jnp
from jax import lax
from jax.sharding import Mesh, PartitionSpec as P

ALL = ("rep", "node", "x", "half")


def partner_pairs(reps):
    ring = 2 * reps
    step = reps // 2
    pairs = []
    for z in range(ring):
        other = z + step if (z // step) % 2 == 1 else z - step
        other %= ring
        pairs.append(((z % reps) * 2 + z // reps, (other % reps) * 2 + other // reps))
    return pairs


def ring(size, step):
    return [(i, (i + step) % size) for i in range(size)]


def on_device(activations, cotangent, gates, experts, groups, weights):
    reps = lax.axis_size("rep")
    nodes = lax.axis_size("node")
    xs = lax.axis_size("x")
    locals_ = xs * lax.axis_size("half")
    tokens, width = activations.shape
    hidden = weights.shape[2]
    slots = experts.shape[1]
    named = groups.shape[1]
    per_group = slots // named
    block = nodes // named
    blocks = tokens // block
    rows_one = nodes * blocks
    cap = max(rows_one // 3, (per_group * rows_one + locals_ - 1) // locals_)
    total = nodes * locals_
    bf = jnp.bfloat16
    f32 = jnp.float32
    pairs = partner_pairs(reps)
    rep_at = lax.axis_index("rep")
    node_at = lax.axis_index("node")
    x_at = lax.axis_index("x")
    half_at = lax.axis_index("half")

    expert_full = jnp.repeat(groups, per_group, axis=1) * locals_ + experts
    gate_wide = jnp.sum(
        jnp.where(
            expert_full[:, :, None] == jnp.arange(total, dtype=jnp.int32)[None, None, :],
            gates.astype(f32)[:, :, None],
            0.0,
        ),
        axis=1,
    ).astype(bf)
    own = jnp.concatenate([activations, cotangent, gate_wide], axis=1)
    wide = own.shape[1]
    other = lax.ppermute(own, ("rep", "half"), pairs)
    both = jnp.concatenate([own, other], axis=0)

    places = 2 * rows_one
    place_index = jnp.arange(places, dtype=jnp.int32)
    place_expert = (
        (place_index // (2 * blocks))[:, None]
        == (jnp.arange(total, dtype=jnp.int32) // locals_)[None, :]
    ).astype(bf)
    named_both = (both[:, width + hidden :] != 0).astype(bf)
    hit = lax.dot_general(
        place_expert, named_both, (((1,), (1,)), ((), ())), preferred_element_type=f32
    )
    placing = (
        (hit > 0)
        & (
            (place_index % (2 * blocks))[:, None]
            == (jnp.arange(2 * tokens, dtype=jnp.int32) // block)[None, :]
        )
    ).astype(bf)
    send_rows = jnp.dot(placing, both, preferred_element_type=f32).astype(bf)
    rows = lax.all_to_all(
        send_rows.reshape(nodes, 2 * blocks, wide), "node", 0, 0, tiled=True
    ).reshape(places, wide)

    cap2 = 2 * cap
    before = (place_index[:, None] < place_index[None, :]).astype(bf)
    slot_at = jnp.arange(cap2, dtype=jnp.int32).astype(f32)

    def pickers(named_here):
        result = []
        for j in range(xs):
            mine_local = jnp.arange(named_here.shape[-1]) == (x_at + j) % xs * 2 + half_at
            live = jnp.sum(jnp.where(mine_local, named_here, 0.0), axis=-1)
            rank = jnp.dot(live.astype(bf), before, preferred_element_type=f32)
            result.append(
                ((live[..., None, :] > 0) & (rank[..., None, :] == slot_at[:, None])).astype(bf)
            )
        return result

    group_gates = lax.dynamic_slice_in_dim(rows, width + hidden + node_at * locals_, locals_, 1)
    picker = pickers((group_gates != 0).astype(f32))
    sent = [jnp.dot(p, rows, preferred_element_type=f32).astype(bf) for p in picker]
    inside = jnp.concatenate(
        [sent[0]] + [lax.ppermute(sent[j], "x", ring(xs, j)) for j in range(1, xs)], axis=0
    )
    taken = xs * cap2

    share = width // reps
    spare = -(share + locals_) % 128
    cols = jnp.stack(
        [
            jnp.concatenate(
                [
                    rows[:, k * share : (k + 1) * share],
                    group_gates,
                    jnp.zeros((places, spare), bf),
                ],
                axis=1,
            )
            for k in range(reps)
        ]
    )
    cols = lax.all_to_all(cols, "rep", 0, 0, tiled=True)

    exp_x = inside[:, :width]
    exp_dy = inside[:, width : width + hidden].astype(f32)
    mine = jnp.arange(total, dtype=jnp.int32) == node_at * locals_ + x_at * 2 + half_at
    gate = jnp.sum(
        jnp.where(mine[None, :], inside[:, width + hidden :].astype(f32), 0.0), axis=1, keepdims=True
    )
    weight = weights[0]
    pre = jnp.dot(exp_x, weight, preferred_element_type=f32)
    sig = jax.nn.sigmoid(pre)
    act = (pre * sig).astype(bf).astype(f32)
    slope = sig * (1.0 + pre * (1.0 - sig))
    grad_pre = (gate * exp_dy * slope).astype(bf)
    grad_in = lax.dot_general(
        grad_pre, weight, (((1,), (1,)), ((), ())), preferred_element_type=f32
    ).astype(bf)
    grad_gate = jnp.sum(exp_dy * act, axis=1, keepdims=True)
    back = jnp.concatenate(
        [
            grad_in,
            (gate * act).astype(bf),
            jnp.where(mine[None, :], grad_gate, 0.0).astype(bf),
        ],
        axis=1,
    )

    gathered = lax.all_gather(grad_pre, "rep", axis=0, tiled=True)

    back_slots = jnp.concatenate(
        [back[:cap2]]
        + [
            lax.ppermute(back[j * cap2 : (j + 1) * cap2], "x", ring(xs, -j))
            for j in range(1, xs)
        ],
        axis=0,
    )
    back_rows = lax.dot_general(
        jnp.concatenate(picker, axis=0),
        back_slots,
        (((0,), (0,)), ((), ())),
        preferred_element_type=f32,
    ).astype(bf)
    back_rows, cols = lax.optimization_barrier((back_rows, cols))
    home_rows = lax.all_to_all(
        back_rows.reshape(nodes, 2 * blocks, wide), "node", 0, 0, tiled=True
    ).reshape(places, wide)

    share_sent = [
        jnp.einsum(
            "pcr,prd->pcd", p, cols[:, :, :share], preferred_element_type=f32
        ).astype(bf)
        for p in pickers((cols[:, :, share : share + locals_] != 0).astype(f32))
    ]
    share_rows = [share_sent[0]] + [
        lax.ppermute(share_sent[j], "x", ring(xs, j)) for j in range(1, xs)
    ]
    home_rows, share_rows = lax.optimization_barrier((home_rows, share_rows))
    x_cols = jnp.stack(share_rows, axis=1).reshape(reps * taken, share)
    grad_share = lax.dot_general(
        x_cols, gathered, (((0,), (0,)), ((), ())), preferred_element_type=f32
    )
    home = lax.dot_general(
        placing, home_rows, (((0,), (0,)), ((), ())), preferred_element_type=f32
    )
    returned = lax.ppermute(home[tokens:].astype(bf), ("rep", "half"), pairs)
    result = home[:tokens] + returned.astype(f32)
    grad_activations = result[:, :width].astype(bf)
    output = result[:, width : width + hidden].astype(bf)
    gate_back = result[:, width + hidden :]
    grad_gates = jnp.sum(
        jnp.where(
            expert_full[:, :, None] == jnp.arange(total, dtype=jnp.int32)[None, None, :],
            gate_back[:, None, :],
            0.0,
        ),
        axis=2,
    ).astype(bf)
    return (output, grad_activations, grad_gates, grad_share[None])


def solution(mesh):
    reps, nodes, locals_ = (mesh.shape[name] for name in ("rep", "node", "local"))
    fine = Mesh(mesh.devices.reshape(reps, nodes, locals_ // 2, 2), ALL)
    rows = P(ALL, None)
    return jax.shard_map(
        on_device,
        mesh=fine,
        in_specs=(rows, rows, rows, rows, rows, P(("node", "x", "half"), None, None)),
        out_specs=(rows, rows, rows, P(("node", "x", "half"), "rep", None)),
        check_vma=False,
    )
```

```python
import jax
import jax.numpy as jnp
from jax import lax
from jax.sharding import Mesh, PartitionSpec as P

ALL = ("rep", "node", "x", "half")


def partner_pairs(reps):
    ring = 2 * reps
    step = reps // 2
    pairs = []
    for z in range(ring):
        other = z + step if (z // step) % 2 == 1 else z - step
        other %= ring
        pairs.append(((z % reps) * 2 + z // reps, (other % reps) * 2 + other // reps))
    return pairs


def ring(size, step):
    return [(i, (i + step) % size) for i in range(size)]


def on_device(activations, cotangent, gates, experts, groups, weights):
    reps = lax.axis_size("rep")
    nodes = lax.axis_size("node")
    xs = lax.axis_size("x")
    locals_ = xs * lax.axis_size("half")
    tokens, width = activations.shape
    hidden = weights.shape[2]
    slots = experts.shape[1]
    named = groups.shape[1]
    per_group = slots // named
    block = nodes // named
    blocks = tokens // block
    rows_one = nodes * blocks
    cap = max(rows_one // 3, (per_group * rows_one + locals_ - 1) // locals_)
    total = nodes * locals_
    bf = jnp.bfloat16
    f32 = jnp.float32
    pairs = partner_pairs(reps)
    rep_at = lax.axis_index("rep")
    node_at = lax.axis_index("node")
    x_at = lax.axis_index("x")
    half_at = lax.axis_index("half")

    expert_full = jnp.repeat(groups, per_group, axis=1) * locals_ + experts
    gate_wide = jnp.sum(
        jnp.where(
            expert_full[:, :, None] == jnp.arange(total, dtype=jnp.int32)[None, None, :],
            gates.astype(f32)[:, :, None],
            0.0,
        ),
        axis=1,
    ).astype(bf)
    own = jnp.concatenate([cotangent, activations, gate_wide], axis=1)
    wide = own.shape[1]
    other = lax.ppermute(own, ("rep", "half"), pairs)
    own, other = lax.optimization_barrier((own, other))
    along_z = lax.all_gather(own[:, hidden:], ("rep", "half"), axis=0, tiled=True)
    both = jnp.concatenate([own, other], axis=0)

    places = 2 * rows_one
    place_index = jnp.arange(places, dtype=jnp.int32)
    place_expert = (
        (place_index // (2 * blocks))[:, None]
        == (jnp.arange(total, dtype=jnp.int32) // locals_)[None, :]
    ).astype(bf)
    named_both = (both[:, width + hidden :] != 0).astype(bf)
    hit = lax.dot_general(
        place_expert, named_both, (((1,), (1,)), ((), ())), preferred_element_type=f32
    )
    placing = (
        (hit > 0)
        & (
            (place_index % (2 * blocks))[:, None]
            == (jnp.arange(2 * tokens, dtype=jnp.int32) // block)[None, :]
        )
    ).astype(bf)
    send_rows = jnp.dot(placing, both, preferred_element_type=f32).astype(bf)
    rows = lax.all_to_all(
        send_rows.reshape(nodes, 2 * blocks, wide), "node", 0, 0, tiled=True
    ).reshape(places, wide)

    cap2 = 2 * cap
    before = (place_index[:, None] < place_index[None, :]).astype(bf)
    slot_at = jnp.arange(cap2, dtype=jnp.int32).astype(f32)

    def pickers(gates_here):
        named_here = (gates_here != 0).astype(f32)
        result = []
        for j in range(xs):
            mine_local = jnp.arange(locals_) == (x_at + j) % xs * 2 + half_at
            live = jnp.sum(jnp.where(mine_local[:, None], named_here, 0.0), axis=-2)
            rank = jnp.dot(live.astype(bf), before, preferred_element_type=f32)
            result.append(
                ((live[..., None, :] > 0) & (rank[..., None, :] == slot_at[:, None])).astype(bf)
            )
        return result

    share = width // reps
    group_expert = (
        (node_at * locals_ + jnp.arange(locals_, dtype=jnp.int32))[:, None]
        == jnp.arange(total, dtype=jnp.int32)[None, :]
    ).astype(bf)
    group_gates = lax.dot_general(
        group_expert,
        rows[:, width + hidden :],
        (((1,), (1,)), ((), ())),
        preferred_element_type=f32,
    ).astype(bf)
    ring_rows = reps * 2 * blocks
    row_index = jnp.arange(nodes * ring_rows, dtype=jnp.int32)
    token_index = jnp.arange(reps * 2 * tokens, dtype=jnp.int32)
    token_rep = token_index // (2 * tokens)
    token_block = token_index % tokens // block
    token_place = jnp.where(
        token_index // tokens % 2 == half_at,
        token_rep * 2 * blocks + token_block,
        (token_rep + reps // 2) % reps * 2 * blocks + blocks + token_block,
    )
    expert_index = jnp.arange(total, dtype=jnp.int32)
    row_expert = (row_index // ring_rows)[:, None] == (expert_index // locals_)[None, :]
    ring_gates = along_z[:, width:]
    row_hit = lax.dot_general(
        row_expert.astype(bf),
        (ring_gates != 0).astype(bf),
        (((1,), (1,)), ((), ())),
        preferred_element_type=f32,
    )
    ring_placing = (
        (row_hit > 0) & ((row_index % ring_rows)[:, None] == token_place[None, :])
    ).astype(bf)
    spare = -share % 128
    fold = ((expert_index % locals_)[:, None] == jnp.arange(spare)[None, :]).astype(bf)
    row_gates = jnp.where(
        row_expert, jnp.dot(ring_placing, ring_gates, preferred_element_type=f32), 0.0
    ).astype(bf)
    cols = jnp.concatenate(
        [
            jnp.dot(
                ring_placing,
                lax.dynamic_slice_in_dim(along_z, rep_at * share, share, 1),
                preferred_element_type=f32,
            ),
            jnp.dot(row_gates, fold, preferred_element_type=f32),
        ],
        axis=1,
    ).astype(bf)

    picker = pickers(group_gates)
    sent = [
        jnp.dot(p, rows, preferred_element_type=f32).astype(bf) for p in picker[1:]
    ]
    moved = [lax.ppermute(sent[j - 1], "x", ring(xs, j)) for j in range(1, xs)]
    kept, cols = lax.optimization_barrier((picker[0], cols))
    inside = jnp.concatenate(
        [jnp.dot(kept, rows, preferred_element_type=f32).astype(bf)] + moved, axis=0
    )
    taken = xs * cap2
    cols = lax.all_to_all(
        cols.reshape(nodes, ring_rows, share + spare), "node", 0, 0, tiled=True
    )

    exp_x = inside[:, hidden : hidden + width]
    exp_dy = inside[:, :hidden].astype(f32)
    mine = jnp.arange(total, dtype=jnp.int32) == node_at * locals_ + x_at * 2 + half_at
    gate = jnp.sum(
        jnp.where(mine[None, :], inside[:, width + hidden :].astype(f32), 0.0), axis=1, keepdims=True
    )
    weight = weights[0]
    pre = jnp.dot(exp_x, weight, preferred_element_type=f32)
    sig = jax.nn.sigmoid(pre)
    act = (pre * sig).astype(bf).astype(f32)
    slope = sig * (1.0 + pre * (1.0 - sig))
    grad_pre = (gate * exp_dy * slope).astype(bf)
    grad_in = lax.dot_general(
        grad_pre, weight, (((1,), (1,)), ((), ())), preferred_element_type=f32
    ).astype(bf)
    grad_gate = jnp.sum(exp_dy * act, axis=1, keepdims=True)
    back = jnp.concatenate(
        [
            (gate * act).astype(bf),
            grad_in,
            jnp.where(mine[None, :], grad_gate, 0.0).astype(bf),
        ],
        axis=1,
    )

    gathered = lax.all_gather(grad_pre, "rep", axis=0, tiled=True)

    back_slots = jnp.concatenate(
        [back[:cap2]]
        + [
            lax.ppermute(back[j * cap2 : (j + 1) * cap2], "x", ring(xs, -j))
            for j in range(1, xs)
        ],
        axis=0,
    )
    back_rows = lax.dot_general(
        jnp.concatenate(picker, axis=0),
        back_slots,
        (((0,), (0,)), ((), ())),
        preferred_element_type=f32,
    ).astype(bf)
    back_rows, cols = lax.optimization_barrier((back_rows, cols))
    home_rows = lax.all_to_all(
        back_rows.reshape(nodes, 2 * blocks, wide), "node", 0, 0, tiled=True
    ).reshape(places, wide)

    cols = (
        cols.reshape(nodes, reps, 2 * blocks, share + spare)
        .transpose(1, 0, 2, 3)
        .reshape(reps, places, share + spare)
    )
    gate_lane = (
        share + jnp.arange(locals_, dtype=jnp.int32)[:, None]
        == jnp.arange(share + spare, dtype=jnp.int32)[None, :]
    ).astype(bf)
    all_gates = jnp.einsum("lc,prc->plr", gate_lane, cols, preferred_element_type=f32)
    share_sent = [
        jnp.einsum("pcr,prd->pcd", p, cols, preferred_element_type=f32).astype(bf)
        for p in pickers(all_gates)
    ]
    share_rows = [share_sent[0]] + [
        lax.ppermute(share_sent[j], "x", ring(xs, j)) for j in range(1, xs)
    ]
    home_rows, share_rows, gathered = lax.optimization_barrier((home_rows, share_rows, gathered))
    x_cols = jnp.stack(share_rows, axis=1).reshape(reps * taken, cols.shape[2])
    x_cols = x_cols[:, :share]
    grad_share = lax.dot_general(
        x_cols, gathered, (((0,), (0,)), ((), ())), preferred_element_type=f32
    )
    home = lax.dot_general(
        placing, home_rows, (((0,), (0,)), ((), ())), preferred_element_type=f32
    )
    returned = lax.ppermute(home[tokens:].astype(bf), ("rep", "half"), pairs)
    result = home[:tokens] + returned.astype(f32)
    grad_activations = result[:, hidden : hidden + width].astype(bf)
    output = result[:, :hidden].astype(bf)
    gate_back = result[:, width + hidden :]
    grad_gates = jnp.sum(
        jnp.where(
            expert_full[:, :, None] == jnp.arange(total, dtype=jnp.int32)[None, None, :],
            gate_back[:, None, :],
            0.0,
        ),
        axis=2,
    ).astype(bf)
    return (output, grad_activations, grad_gates, grad_share[None])


def solution(mesh):
    reps, nodes, locals_ = (mesh.shape[name] for name in ("rep", "node", "local"))
    fine = Mesh(mesh.devices.reshape(reps, nodes, locals_ // 2, 2), ALL)
    rows = P(ALL, None)
    return jax.shard_map(
        on_device,
        mesh=fine,
        in_specs=(rows, rows, rows, rows, rows, P(("node", "x", "half"), None, None)),
        out_specs=(rows, rows, rows, P(("node", "x", "half"), "rep", None)),
        check_vma=False,
    )
```

```python
import functools

import jax
import jax.numpy as jnp
from jax import lax
from jax.experimental import pallas as pl
from jax.experimental.pallas import tpu as pltpu
from jax.sharding import Mesh, PartitionSpec as P

ALL = ("rep", "node", "x", "half")


def partner_pairs(reps):
    ring = 2 * reps
    step = reps // 2
    pairs = []
    for z in range(ring):
        other = z + step if (z // step) % 2 == 1 else z - step
        other %= ring
        pairs.append(((z % reps) * 2 + z // reps, (other % reps) * 2 + other // reps))
    return pairs


def ring(size, step):
    return [(i, (i + step) % size) for i in range(size)]


def expert_kernel(hidden, width, chunk, mine_ref, *refs):
    count = (len(refs) - 5) // 2
    slabs, weight_ref = refs[:count], refs[count]
    backs, grad_ref = refs[count + 1 : 2 * count + 1], refs[2 * count + 1]
    held, total, sems = refs[2 * count + 2 :]
    rows = slabs[0].shape[0]
    chunks = width // chunk
    f32 = jnp.float32
    bf = jnp.bfloat16
    copies = [
        pltpu.make_async_copy(
            weight_ref.at[0, pl.ds(k * chunk, chunk), :],
            held.at[pl.ds(k * chunk, chunk), :],
            sems.at[k],
        )
        for k in range(chunks)
    ]
    for copy in copies:
        copy.start()

    def gather(start, size):
        return jnp.concatenate([slab[:, start : start + size] for slab in slabs], axis=0)

    for k in range(chunks):
        copies[k].wait()
        part = jnp.dot(
            gather(hidden + k * chunk, chunk),
            held[k * chunk : (k + 1) * chunk, :],
            preferred_element_type=f32,
        )
        if k:
            total[...] += part
        else:
            total[...] = part
    mine = mine_ref[...]
    gate = jnp.sum(
        gather(hidden + width, mine.shape[1]).astype(f32) * mine, axis=1, keepdims=True
    )
    pre = total[...]
    dy = gather(0, hidden).astype(f32)
    sig = jax.nn.sigmoid(pre)
    act = (pre * sig).astype(bf).astype(f32)
    grad_pre = (gate * dy * (sig * (1.0 + pre * (1.0 - sig)))).astype(bf)
    grad_ref[...] = grad_pre
    grad_gate = (jnp.sum(dy * act, axis=1, keepdims=True) * mine).astype(bf)
    scaled = (gate * act).astype(bf)
    for j, back in enumerate(backs):
        back[:, :hidden] = scaled[j * rows : (j + 1) * rows]
        back[:, hidden + width :] = grad_gate[j * rows : (j + 1) * rows]
    for k in range(chunks):
        part = lax.dot_general(
            grad_pre,
            held[k * chunk : (k + 1) * chunk, :],
            (((1,), (1,)), ((), ())),
            preferred_element_type=f32,
        ).astype(bf)
        for j, back in enumerate(backs):
            back[:, hidden + k * chunk : hidden + (k + 1) * chunk] = part[
                j * rows : (j + 1) * rows
            ]


def expert(slabs, weights, mine):
    rows, wide = slabs[0].shape
    width, hidden = weights.shape[1:]
    chunk = 512 if width % 512 == 0 else width
    count = len(slabs)
    vmem = pl.BlockSpec(memory_space=pltpu.VMEM)
    result = pl.pallas_call(
        functools.partial(expert_kernel, hidden, width, chunk),
        out_shape=[jax.ShapeDtypeStruct((rows, wide), jnp.bfloat16)] * count
        + [jax.ShapeDtypeStruct((count * rows, hidden), jnp.bfloat16)],
        in_specs=[vmem] * (count + 1) + [pl.BlockSpec(memory_space=pl.ANY)],
        out_specs=[vmem] * (count + 1),
        scratch_shapes=[
            pltpu.VMEM((width, hidden), jnp.bfloat16),
            pltpu.VMEM((count * rows, hidden), jnp.float32),
            pltpu.SemaphoreType.DMA((width // chunk,)),
        ],
        compiler_params=pltpu.CompilerParams(vmem_limit_bytes=32 * 1024 * 1024),
        cost_estimate=pl.CostEstimate(flops=0, bytes_accessed=1024, transcendentals=0),
    )(mine, *slabs, weights)
    return result[:count], result[count]


def on_device(activations, cotangent, gates, experts, groups, weights):
    reps = lax.axis_size("rep")
    nodes = lax.axis_size("node")
    xs = lax.axis_size("x")
    locals_ = xs * lax.axis_size("half")
    tokens, width = activations.shape
    hidden = weights.shape[2]
    slots = experts.shape[1]
    named = groups.shape[1]
    per_group = slots // named
    block = nodes // named
    blocks = tokens // block
    rows_one = nodes * blocks
    cap = max(rows_one // 3, (per_group * rows_one + locals_ - 1) // locals_)
    total = nodes * locals_
    bf = jnp.bfloat16
    f32 = jnp.float32
    pairs = partner_pairs(reps)
    rep_at = lax.axis_index("rep")
    node_at = lax.axis_index("node")
    x_at = lax.axis_index("x")
    half_at = lax.axis_index("half")

    expert_full = jnp.repeat(groups, per_group, axis=1) * locals_ + experts
    gate_wide = jnp.sum(
        jnp.where(
            expert_full[:, :, None] == jnp.arange(total, dtype=jnp.int32)[None, None, :],
            gates.astype(f32)[:, :, None],
            0.0,
        ),
        axis=1,
    ).astype(bf)
    own = jnp.concatenate([cotangent, activations, gate_wide], axis=1)
    wide = own.shape[1]
    other = lax.ppermute(own, ("rep", "half"), pairs)
    own, other = lax.optimization_barrier((own, other))
    along_z = lax.all_gather(own[:, hidden:], ("half", "rep"), axis=0, tiled=True)
    both = jnp.concatenate([own, other], axis=0)

    places = 2 * rows_one
    place_index = jnp.arange(places, dtype=jnp.int32)
    place_expert = (
        (place_index // (2 * blocks))[:, None]
        == (jnp.arange(total, dtype=jnp.int32) // locals_)[None, :]
    ).astype(bf)
    named_both = (both[:, width + hidden :] != 0).astype(bf)
    hit = lax.dot_general(
        place_expert, named_both, (((1,), (1,)), ((), ())), preferred_element_type=f32
    )
    placing = (
        (hit > 0)
        & (
            (place_index % (2 * blocks))[:, None]
            == (jnp.arange(2 * tokens, dtype=jnp.int32) // block)[None, :]
        )
    ).astype(bf)
    send_rows = jnp.dot(placing, both, preferred_element_type=f32).astype(bf)
    rows = lax.all_to_all(
        send_rows.reshape(nodes, 2 * blocks, wide), "node", 0, 0, tiled=True
    ).reshape(places, wide)

    cap2 = -(-2 * cap // 16) * 16
    before = (place_index[:, None] < place_index[None, :]).astype(bf)
    slot_at = jnp.arange(cap2, dtype=jnp.int32).astype(f32)

    def pickers(gates_here):
        named_here = (gates_here != 0).astype(f32)
        result = []
        for j in range(xs):
            mine_local = jnp.arange(locals_) == (x_at + j) % xs * 2 + half_at
            live = jnp.sum(jnp.where(mine_local[:, None], named_here, 0.0), axis=-2)
            rank = jnp.dot(live.astype(bf), before, preferred_element_type=f32)
            result.append(
                ((live[..., None, :] > 0) & (rank[..., None, :] == slot_at[:, None])).astype(bf)
            )
        return result

    share = width // reps
    group_expert = (
        (node_at * locals_ + jnp.arange(locals_, dtype=jnp.int32))[:, None]
        == jnp.arange(total, dtype=jnp.int32)[None, :]
    ).astype(bf)
    group_gates = lax.dot_general(
        group_expert,
        rows[:, width + hidden :],
        (((1,), (1,)), ((), ())),
        preferred_element_type=f32,
    ).astype(bf)
    ring_rows = reps * 2 * blocks
    row_index = jnp.arange(nodes * ring_rows, dtype=jnp.int32)
    token_index = jnp.arange(reps * 2 * tokens, dtype=jnp.int32)
    token_rep = token_index // tokens % reps
    token_block = token_index % tokens // block
    token_place = jnp.where(
        token_index // (tokens * reps) == half_at,
        token_rep * 2 * blocks + token_block,
        (token_rep + reps // 2) % reps * 2 * blocks + blocks + token_block,
    )
    expert_index = jnp.arange(total, dtype=jnp.int32)
    row_expert = (row_index // ring_rows)[:, None] == (expert_index // locals_)[None, :]
    ring_gates = along_z[:, width:]
    row_hit = lax.dot_general(
        row_expert.astype(bf),
        (ring_gates != 0).astype(bf),
        (((1,), (1,)), ((), ())),
        preferred_element_type=f32,
    )
    ring_placing = (
        (row_hit > 0) & ((row_index % ring_rows)[:, None] == token_place[None, :])
    ).astype(bf)
    spare = -share % 128
    fold = ((expert_index % locals_)[:, None] == jnp.arange(spare)[None, :]).astype(bf)
    row_gates = jnp.where(
        row_expert, jnp.dot(ring_placing, ring_gates, preferred_element_type=f32), 0.0
    ).astype(bf)
    cols = jnp.concatenate(
        [
            jnp.dot(
                ring_placing,
                lax.dynamic_slice_in_dim(along_z, rep_at * share, share, 1),
                preferred_element_type=f32,
            ),
            jnp.dot(row_gates, fold, preferred_element_type=f32),
        ],
        axis=1,
    ).astype(bf)

    picker = pickers(group_gates)
    sent = [
        jnp.dot(p, rows, preferred_element_type=f32).astype(bf) for p in picker[1:]
    ]
    moved = [lax.ppermute(sent[j - 1], "x", ring(xs, j)) for j in range(1, xs)]
    kept, cols = lax.optimization_barrier((picker[0], cols))
    slabs = [jnp.dot(kept, rows, preferred_element_type=f32).astype(bf)] + moved
    taken = xs * cap2
    cols = lax.all_to_all(
        cols.reshape(nodes, ring_rows, share + spare), "node", 0, 0, tiled=True
    )

    mine = jnp.arange(total, dtype=jnp.int32) == node_at * locals_ + x_at * 2 + half_at
    back, grad_pre = expert(slabs, weights, mine.astype(f32)[None, :])

    gathered = lax.all_gather(grad_pre, "rep", axis=0, tiled=True)

    last = xs - 1
    back_last, cols = lax.optimization_barrier((back[last], cols))
    back_slots = jnp.concatenate(
        [back[0]]
        + [
            lax.ppermute(back_last if j == last else back[j], "x", ring(xs, -j))
            for j in range(1, xs)
        ],
        axis=0,
    )
    back_rows = lax.dot_general(
        jnp.concatenate(picker, axis=0),
        back_slots,
        (((0,), (0,)), ((), ())),
        preferred_element_type=f32,
    ).astype(bf)
    home_rows = lax.all_to_all(
        back_rows.reshape(nodes, 2 * blocks, wide), "node", 0, 0, tiled=True
    ).reshape(places, wide)

    cols = (
        cols.reshape(nodes, reps, 2 * blocks, share + spare)
        .transpose(1, 0, 2, 3)
        .reshape(reps, places, share + spare)
    )
    gate_lane = (
        share + jnp.arange(locals_, dtype=jnp.int32)[:, None]
        == jnp.arange(share + spare, dtype=jnp.int32)[None, :]
    ).astype(bf)
    all_gates = jnp.einsum("lc,prc->plr", gate_lane, cols, preferred_element_type=f32)
    share_sent = [
        jnp.einsum("pcr,prd->pcd", p, cols, preferred_element_type=f32).astype(bf)
        for p in pickers(all_gates)
    ]
    share_rows = [share_sent[0]] + [
        lax.ppermute(share_sent[j], "x", ring(xs, j)) for j in range(1, xs)
    ]
    x_cols = jnp.stack(share_rows, axis=1).reshape(reps * taken, cols.shape[2])
    x_cols = x_cols[:, :share]
    grad_share = lax.dot_general(
        x_cols, gathered, (((0,), (0,)), ((), ())), preferred_element_type=f32
    )
    home = lax.dot_general(
        placing, home_rows, (((0,), (0,)), ((), ())), preferred_element_type=f32
    )
    returned = lax.ppermute(home[tokens:].astype(bf), ("rep", "half"), pairs)
    returned, grad_share = lax.optimization_barrier((returned, grad_share))
    result = home[:tokens] + returned.astype(f32)
    grad_activations = result[:, hidden : hidden + width].astype(bf)
    output = result[:, :hidden].astype(bf)
    gate_back = result[:, width + hidden :]
    grad_gates = jnp.sum(
        jnp.where(
            expert_full[:, :, None] == jnp.arange(total, dtype=jnp.int32)[None, None, :],
            gate_back[:, None, :],
            0.0,
        ),
        axis=2,
    ).astype(bf)
    return (output, grad_activations, grad_gates, grad_share[None])


def solution(mesh):
    reps, nodes, locals_ = (mesh.shape[name] for name in ("rep", "node", "local"))
    fine = Mesh(mesh.devices.reshape(reps, nodes, locals_ // 2, 2), ALL)
    rows = P(ALL, None)
    return jax.shard_map(
        on_device,
        mesh=fine,
        in_specs=(rows, rows, rows, rows, rows, P(("node", "x", "half"), None, None)),
        out_specs=(rows, rows, rows, P(("node", "x", "half"), "rep", None)),
        check_vma=False,
    )
```

```python
import functools

import jax
import jax.numpy as jnp
from jax import lax
from jax.experimental import pallas as pl
from jax.experimental.pallas import tpu as pltpu
from jax.sharding import Mesh, PartitionSpec as P

ALL = ("rep", "node", "x", "half")


def partner_pairs(reps):
    ring = 2 * reps
    step = reps // 2
    pairs = []
    for z in range(ring):
        other = z + step if (z // step) % 2 == 1 else z - step
        other %= ring
        pairs.append(((z % reps) * 2 + z // reps, (other % reps) * 2 + other // reps))
    return pairs


def ring(size, step):
    return [(i, (i + step) % size) for i in range(size)]


def expert_kernel(hidden, width, chunk, mine_ref, *refs):
    count = (len(refs) - 5) // 2
    slabs, weight_ref = refs[:count], refs[count]
    backs, grad_ref = refs[count + 1 : 2 * count + 1], refs[2 * count + 1]
    held, total, sems = refs[2 * count + 2 :]
    rows = slabs[0].shape[0]
    chunks = width // chunk
    f32 = jnp.float32
    bf = jnp.bfloat16
    copies = [
        pltpu.make_async_copy(
            weight_ref.at[0, pl.ds(k * chunk, chunk), :],
            held.at[pl.ds(k * chunk, chunk), :],
            sems.at[k],
        )
        for k in range(chunks)
    ]
    for copy in copies:
        copy.start()

    def gather(start, size):
        return jnp.concatenate([slab[:, start : start + size] for slab in slabs], axis=0)

    for k in range(chunks):
        copies[k].wait()
        part = jnp.dot(
            gather(hidden + k * chunk, chunk),
            held[k * chunk : (k + 1) * chunk, :],
            preferred_element_type=f32,
        )
        if k:
            total[...] += part
        else:
            total[...] = part
    mine = mine_ref[...]
    gate = jnp.sum(
        gather(hidden + width, mine.shape[1]).astype(f32) * mine, axis=1, keepdims=True
    )
    pre = total[...]
    dy = gather(0, hidden).astype(f32)
    sig = jax.nn.sigmoid(pre)
    act = (pre * sig).astype(bf).astype(f32)
    grad_pre = (gate * dy * (sig * (1.0 + pre * (1.0 - sig)))).astype(bf)
    grad_ref[...] = grad_pre
    grad_gate = (jnp.sum(dy * act, axis=1, keepdims=True) * mine).astype(bf)
    scaled = (gate * act).astype(bf)
    for j, back in enumerate(backs):
        back[:, :hidden] = scaled[j * rows : (j + 1) * rows]
        back[:, hidden + width :] = grad_gate[j * rows : (j + 1) * rows]
    for k in range(chunks):
        part = lax.dot_general(
            grad_pre,
            held[k * chunk : (k + 1) * chunk, :],
            (((1,), (1,)), ((), ())),
            preferred_element_type=f32,
        ).astype(bf)
        for j, back in enumerate(backs):
            back[:, hidden + k * chunk : hidden + (k + 1) * chunk] = part[
                j * rows : (j + 1) * rows
            ]


def expert(slabs, weights, mine):
    rows, wide = slabs[0].shape
    width, hidden = weights.shape[1:]
    chunk = 512 if width % 512 == 0 else width
    count = len(slabs)
    vmem = pl.BlockSpec(memory_space=pltpu.VMEM)
    result = pl.pallas_call(
        functools.partial(expert_kernel, hidden, width, chunk),
        out_shape=[jax.ShapeDtypeStruct((rows, wide), jnp.bfloat16)] * count
        + [jax.ShapeDtypeStruct((count * rows, hidden), jnp.bfloat16)],
        in_specs=[vmem] * (count + 1) + [pl.BlockSpec(memory_space=pl.ANY)],
        out_specs=[vmem] * (count + 1),
        scratch_shapes=[
            pltpu.VMEM((width, hidden), jnp.bfloat16),
            pltpu.VMEM((count * rows, hidden), jnp.float32),
            pltpu.SemaphoreType.DMA((width // chunk,)),
        ],
        compiler_params=pltpu.CompilerParams(vmem_limit_bytes=32 * 1024 * 1024),
        cost_estimate=pl.CostEstimate(flops=0, bytes_accessed=1024, transcendentals=0),
    )(mine, *slabs, weights)
    return result[:count], result[count]


def window_kernel(width, starts_ref, rows_ref, *refs):
    outs, sems = refs[:-1], refs[-1]
    window = outs[0].shape[1] - rows_ref.shape[1] + width
    first = rows_ref.shape[1] - width
    copies = []
    for k, out in enumerate(outs):
        start = pl.multiple_of(starts_ref[k], 128)
        copies.append(
            pltpu.make_async_copy(
                rows_ref.at[:, pl.ds(start, window)], out.at[:, :window], sems.at[2 * k]
            )
        )
        copies.append(
            pltpu.make_async_copy(
                rows_ref.at[:, pl.ds(width, first)], out.at[:, window:], sems.at[2 * k + 1]
            )
        )
    for copy in copies:
        copy.start()
    for copy in copies:
        copy.wait()


def share_windows(rows, width, window, starts):
    count = starts.shape[0]
    wide = window + rows.shape[1] - width
    return pl.pallas_call(
        functools.partial(window_kernel, width),
        out_shape=[jax.ShapeDtypeStruct((rows.shape[0], wide), rows.dtype)] * count,
        in_specs=[pl.BlockSpec(memory_space=pltpu.SMEM), pl.BlockSpec(memory_space=pl.ANY)],
        out_specs=[pl.BlockSpec(memory_space=pl.ANY)] * count,
        scratch_shapes=[pltpu.SemaphoreType.DMA((2 * count,))],
        cost_estimate=pl.CostEstimate(flops=0, bytes_accessed=1024, transcendentals=0),
    )(starts, rows)


def place_kernel(groups_ref, mask_ref, fold_ref, valid_ref, ends_ref, *refs):
    pieces, out_ref = refs[:-1], refs[-1]
    f32 = jnp.float32
    bf = jnp.bfloat16
    window = out_ref.shape[1]
    tokens = jnp.concatenate([piece[...] for piece in pieces], axis=0)
    gate = tokens[:, window:]
    named = jnp.where(gate.astype(f32) != 0, 1.0, 0.0).astype(bf)
    hits = lax.dot_general(
        groups_ref[...], named, (((1,), (1,)), ((), ())), preferred_element_type=f32
    )
    hits = jnp.where(hits > 0, 1.0, 0.0)
    values = jnp.where(valid_ref[...] > 0, tokens[:, :window].astype(f32), 0.0).astype(bf)
    mask = mask_ref[...].astype(f32)
    group_mask = groups_ref[...].astype(f32)
    fold = fold_ref[...]
    count = groups_ref.shape[0]
    places = mask.shape[0]
    for g in range(0, count, 4):
        placing = jnp.concatenate(
            [mask * hits[g + i : g + i + 1] for i in range(4)], axis=0
        ).astype(bf)
        part = jnp.dot(placing, values, preferred_element_type=f32)
        row_gate = jnp.dot(placing, gate, preferred_element_type=f32)
        row_gate = jnp.concatenate(
            [
                row_gate[i * places : (i + 1) * places] * group_mask[g + i : g + i + 1]
                for i in range(4)
            ],
            axis=0,
        ).astype(bf)
        lanes = jnp.dot(row_gate, fold, preferred_element_type=f32)
        here = slice(g * places, (g + 4) * places)
        if window == 128:
            out_ref[here, :] = (part + lanes).astype(bf)
        else:
            out_ref[here, :128] = (part[:, :128] + lanes * ends_ref[0:1, :]).astype(bf)
            out_ref[here, 128 : window - 128] = part[:, 128 : window - 128].astype(bf)
            out_ref[here, window - 128 :] = (
                part[:, window - 128 :] + lanes * ends_ref[1:2, :]
            ).astype(bf)


def place_columns(pieces, window, groups, mask, fold, valid, ends):
    vmem = pl.BlockSpec(memory_space=pltpu.VMEM)
    return pl.pallas_call(
        place_kernel,
        out_shape=jax.ShapeDtypeStruct((groups.shape[0] * mask.shape[0], window), jnp.bfloat16),
        in_specs=[vmem] * (5 + len(pieces)),
        out_specs=vmem,
        compiler_params=pltpu.CompilerParams(vmem_limit_bytes=24 * 1024 * 1024),
        cost_estimate=pl.CostEstimate(flops=0, bytes_accessed=1024, transcendentals=0),
    )(groups, mask, fold, valid, ends, *pieces)


def on_device(activations, cotangent, gates, experts, groups, weights):
    reps = lax.axis_size("rep")
    nodes = lax.axis_size("node")
    xs = lax.axis_size("x")
    locals_ = xs * lax.axis_size("half")
    tokens, width = activations.shape
    hidden = weights.shape[2]
    slots = experts.shape[1]
    named = groups.shape[1]
    per_group = slots // named
    block = nodes // named
    blocks = tokens // block
    rows_one = nodes * blocks
    cap = max(rows_one // 3, (per_group * rows_one + locals_ - 1) // locals_)
    total = nodes * locals_
    bf = jnp.bfloat16
    f32 = jnp.float32
    pairs = partner_pairs(reps)
    rep_at = lax.axis_index("rep")
    node_at = lax.axis_index("node")
    x_at = lax.axis_index("x")
    half_at = lax.axis_index("half")

    expert_full = jnp.repeat(groups, per_group, axis=1) * locals_ + experts
    gate_wide = jnp.sum(
        jnp.where(
            expert_full[:, :, None] == jnp.arange(total, dtype=jnp.int32)[None, None, :],
            gates.astype(f32)[:, :, None],
            0.0,
        ),
        axis=1,
    ).astype(bf)
    own = jnp.concatenate([cotangent, activations, gate_wide], axis=1)
    wide = own.shape[1]
    other = lax.ppermute(own, ("rep", "half"), pairs)
    both = jnp.concatenate([own, other], axis=0)

    places = 2 * rows_one
    place_index = jnp.arange(places, dtype=jnp.int32)
    place_expert = (
        (place_index // (2 * blocks))[:, None]
        == (jnp.arange(total, dtype=jnp.int32) // locals_)[None, :]
    ).astype(bf)
    named_both = (both[:, width + hidden :] != 0).astype(bf)
    hit = lax.dot_general(
        place_expert, named_both, (((1,), (1,)), ((), ())), preferred_element_type=f32
    )
    placing = (
        (hit > 0)
        & (
            (place_index % (2 * blocks))[:, None]
            == (jnp.arange(2 * tokens, dtype=jnp.int32) // block)[None, :]
        )
    ).astype(bf)
    send_rows = jnp.dot(placing, both, preferred_element_type=f32).astype(bf)
    rows = lax.all_to_all(
        send_rows.reshape(nodes, 2 * blocks, wide), "node", 0, 0, tiled=True
    ).reshape(places, wide)

    filled = 2 * cap
    cap2 = -(-filled // 16) * 16
    before = (place_index[:, None] < place_index[None, :]).astype(bf)
    slot_at = jnp.arange(cap2, dtype=jnp.int32).astype(f32)

    def pickers(gates_here):
        named_here = (gates_here != 0).astype(f32)
        result = []
        for j in range(xs):
            mine_local = jnp.arange(locals_) == (x_at + j) % xs * 2 + half_at
            live = jnp.sum(jnp.where(mine_local[:, None], named_here, 0.0), axis=-2)
            rank = jnp.dot(live.astype(bf), before, preferred_element_type=f32)
            result.append(
                ((live[..., None, :] > 0) & (rank[..., None, :] == slot_at[:, None])).astype(bf)
            )
        return result

    share = width // reps
    group_expert = (
        (node_at * locals_ + jnp.arange(locals_, dtype=jnp.int32))[:, None]
        == jnp.arange(total, dtype=jnp.int32)[None, :]
    ).astype(bf)
    group_gates = lax.dot_general(
        group_expert,
        rows[:, width + hidden :],
        (((1,), (1,)), ((), ())),
        preferred_element_type=f32,
    ).astype(bf)
    ring_rows = reps * 2 * blocks
    window = -(-share // 128) * 128
    offset = rep_at * share % 128
    gate_start = jnp.where(offset == 0, share, 0)
    lane = jnp.arange(window, dtype=jnp.int32)
    steps = jnp.arange(reps, dtype=jnp.int32)
    pieces = share_windows(
        both[:, hidden:], width, window, (rep_at + steps) % reps * share // 128 * 128
    )
    pieces = [pieces[0]] + [
        lax.ppermute(pieces[k], "rep", ring(reps, k)) for k in range(1, reps)
    ]
    token_place = (
        ((rep_at + reps - steps) % reps * 2 * blocks)[:, None]
        + (jnp.arange(2 * tokens, dtype=jnp.int32) // block)[None, :]
    ).reshape(reps * 2 * tokens)
    expert_index = jnp.arange(total, dtype=jnp.int32)
    cols = place_columns(
        pieces,
        window,
        (jnp.arange(nodes)[:, None] == (expert_index // locals_)[None, :]).astype(bf),
        (jnp.arange(ring_rows)[:, None] == token_place[None, :]).astype(bf),
        (
            jnp.arange(128)[None, :] == (gate_start % 128 + expert_index % locals_)[:, None]
        ).astype(bf),
        ((lane >= offset) & (lane < offset + share)).astype(f32)[None, :],
        jnp.stack([jnp.where(offset == 0, 0.0, 1.0), jnp.where(offset == 0, 1.0, 0.0)])[
            :, None
        ]
        * jnp.ones((2, 128), f32),
    )

    rows, group_gates, cols = lax.optimization_barrier((rows, group_gates, cols))
    picker = pickers(group_gates)
    sent = [
        jnp.dot(p, rows, preferred_element_type=f32).astype(bf) for p in picker[1:]
    ]
    moved = [lax.ppermute(sent[j - 1], "x", ring(xs, j)) for j in range(1, xs)]
    kept = picker[0]
    slabs = [jnp.dot(kept, rows, preferred_element_type=f32).astype(bf)] + moved
    cols = lax.all_to_all(
        cols.reshape(nodes, ring_rows, window), "node", 0, 0, tiled=True
    )

    mine = jnp.arange(total, dtype=jnp.int32) == node_at * locals_ + x_at * 2 + half_at
    back, grad_pre = expert(slabs, weights, mine.astype(f32)[None, :])

    grad_pre = grad_pre.reshape(xs, cap2, hidden)[:, :filled].reshape(xs * filled, hidden)
    gathered = lax.all_gather(grad_pre, "rep", axis=0, tiled=True)

    last = xs - 1
    back_last, cols = lax.optimization_barrier((back[last], cols))
    back_slots = jnp.concatenate(
        [back[0]]
        + [
            lax.ppermute(back_last if j == last else back[j], "x", ring(xs, -j))
            for j in range(1, xs)
        ],
        axis=0,
    )
    back_rows = lax.dot_general(
        jnp.concatenate(picker, axis=0),
        back_slots,
        (((0,), (0,)), ((), ())),
        preferred_element_type=f32,
    ).astype(bf)
    home_rows = lax.all_to_all(
        back_rows.reshape(nodes, 2 * blocks, wide), "node", 0, 0, tiled=True
    ).reshape(places, wide)

    cols = (
        cols.reshape(nodes, reps, 2 * blocks, window)
        .transpose(1, 0, 2, 3)
        .reshape(reps, places, window)
    )
    gate_lane = (
        gate_start + jnp.arange(locals_, dtype=jnp.int32)[:, None] == lane[None, :]
    ).astype(bf)
    all_gates = jnp.einsum("lc,prc->plr", gate_lane, cols, preferred_element_type=f32)
    share_sent = [
        jnp.einsum("pcr,prd->pcd", p, cols, preferred_element_type=f32).astype(bf)
        for p in pickers(all_gates)
    ]
    share_rows = [share_sent[0]] + [
        lax.ppermute(share_sent[j], "x", ring(xs, j)) for j in range(1, xs)
    ]
    x_cols = jnp.stack([part[:, :filled] for part in share_rows], axis=1)
    x_cols = lax.dynamic_slice_in_dim(
        x_cols.reshape(reps * xs * filled, window), offset, share, 1
    )
    grad_share = lax.dot_general(
        x_cols, gathered, (((0,), (0,)), ((), ())), preferred_element_type=f32
    )
    home = lax.dot_general(
        placing, home_rows, (((0,), (0,)), ((), ())), preferred_element_type=f32
    )
    returned = lax.ppermute(home[tokens:].astype(bf), ("rep", "half"), pairs)
    returned, grad_share = lax.optimization_barrier((returned, grad_share))
    result = home[:tokens] + returned.astype(f32)
    grad_activations = result[:, hidden : hidden + width].astype(bf)
    output = result[:, :hidden].astype(bf)
    gate_back = result[:, width + hidden :]
    grad_gates = jnp.sum(
        jnp.where(
            expert_full[:, :, None] == jnp.arange(total, dtype=jnp.int32)[None, None, :],
            gate_back[:, None, :],
            0.0,
        ),
        axis=2,
    ).astype(bf)
    return (output, grad_activations, grad_gates, grad_share[None])


def solution(mesh):
    reps, nodes, locals_ = (mesh.shape[name] for name in ("rep", "node", "local"))
    fine = Mesh(mesh.devices.reshape(reps, nodes, locals_ // 2, 2), ALL)
    rows = P(ALL, None)
    return jax.shard_map(
        on_device,
        mesh=fine,
        in_specs=(rows, rows, rows, rows, rows, P(("node", "x", "half"), None, None)),
        out_specs=(rows, rows, rows, P(("node", "x", "half"), "rep", None)),
        check_vma=False,
    )
```

```python
import functools

import jax
import jax.numpy as jnp
from jax import lax
from jax.experimental import pallas as pl
from jax.experimental.pallas import tpu as pltpu
from jax.sharding import Mesh, PartitionSpec as P

ALL = ("rep", "node", "x", "half")


def partner_pairs(reps):
    ring = 2 * reps
    step = reps // 2
    pairs = []
    for z in range(ring):
        other = z + step if (z // step) % 2 == 1 else z - step
        other %= ring
        pairs.append(((z % reps) * 2 + z // reps, (other % reps) * 2 + other // reps))
    return pairs


def ring(size, step):
    return [(i, (i + step) % size) for i in range(size)]


def expert_kernel(hidden, width, chunk, mine_ref, *refs):
    count = (len(refs) - 5) // 2
    slabs, weight_ref = refs[:count], refs[count]
    backs, grad_ref = refs[count + 1 : 2 * count + 1], refs[2 * count + 1]
    held, total, sems = refs[2 * count + 2 :]
    rows = slabs[0].shape[0]
    chunks = width // chunk
    f32 = jnp.float32
    bf = jnp.bfloat16
    copies = [
        pltpu.make_async_copy(
            weight_ref.at[0, pl.ds(k * chunk, chunk), :],
            held.at[pl.ds(k * chunk, chunk), :],
            sems.at[k],
        )
        for k in range(chunks)
    ]
    for copy in copies:
        copy.start()

    def gather(start, size):
        return jnp.concatenate([slab[:, start : start + size] for slab in slabs], axis=0)

    for k in range(chunks):
        copies[k].wait()
        part = jnp.dot(
            gather(hidden + k * chunk, chunk),
            held[k * chunk : (k + 1) * chunk, :],
            preferred_element_type=f32,
        )
        if k:
            total[...] += part
        else:
            total[...] = part
    mine = mine_ref[...]
    gate = jnp.sum(
        gather(hidden + width, mine.shape[1]).astype(f32) * mine, axis=1, keepdims=True
    )
    pre = total[...]
    dy = gather(0, hidden).astype(f32)
    sig = jax.nn.sigmoid(pre)
    act = (pre * sig).astype(bf).astype(f32)
    grad_pre = (gate * dy * (sig * (1.0 + pre * (1.0 - sig)))).astype(bf)
    grad_ref[...] = grad_pre
    grad_gate = (jnp.sum(dy * act, axis=1, keepdims=True) * mine).astype(bf)
    scaled = (gate * act).astype(bf)
    for j, back in enumerate(backs):
        back[:, :hidden] = scaled[j * rows : (j + 1) * rows]
        back[:, hidden + width :] = grad_gate[j * rows : (j + 1) * rows]
    for k in range(chunks):
        part = lax.dot_general(
            grad_pre,
            held[k * chunk : (k + 1) * chunk, :],
            (((1,), (1,)), ((), ())),
            preferred_element_type=f32,
        ).astype(bf)
        for j, back in enumerate(backs):
            back[:, hidden + k * chunk : hidden + (k + 1) * chunk] = part[
                j * rows : (j + 1) * rows
            ]


def expert(slabs, weights, mine):
    rows, wide = slabs[0].shape
    width, hidden = weights.shape[1:]
    chunk = 512 if width % 512 == 0 else width
    count = len(slabs)
    vmem = pl.BlockSpec(memory_space=pltpu.VMEM)
    result = pl.pallas_call(
        functools.partial(expert_kernel, hidden, width, chunk),
        out_shape=[jax.ShapeDtypeStruct((rows, wide), jnp.bfloat16)] * count
        + [jax.ShapeDtypeStruct((count * rows, hidden), jnp.bfloat16)],
        in_specs=[vmem] * (count + 1) + [pl.BlockSpec(memory_space=pl.ANY)],
        out_specs=[vmem] * (count + 1),
        scratch_shapes=[
            pltpu.VMEM((width, hidden), jnp.bfloat16),
            pltpu.VMEM((count * rows, hidden), jnp.float32),
            pltpu.SemaphoreType.DMA((width // chunk,)),
        ],
        compiler_params=pltpu.CompilerParams(vmem_limit_bytes=32 * 1024 * 1024),
        cost_estimate=pl.CostEstimate(flops=0, bytes_accessed=1024, transcendentals=0),
    )(mine, *slabs, weights)
    return result[:count], result[count]


def window_kernel(hidden, width, starts, rows_ref, fold_ref, out_ref):
    f32 = jnp.float32
    bf = jnp.bfloat16
    window = out_ref.shape[2]
    gates = jnp.dot(
        rows_ref[:, hidden + width :], fold_ref[...], preferred_element_type=f32
    )
    lane = lax.broadcasted_iota(jnp.int32, gates.shape, 1)
    for k, (start, spare_first) in enumerate(starts):
        at = hidden + start
        if spare_first:
            edge = jnp.where(lane < 64, gates, rows_ref[:, at : at + 128].astype(f32))
            out_ref[k, :, :128] = edge.astype(bf)
            if window > 128:
                out_ref[k, :, 128:] = rows_ref[:, at + 128 : at + window]
        else:
            last = at + window - 128
            edge = jnp.where(lane < 64, rows_ref[:, last : last + 128].astype(f32), gates)
            out_ref[k, :, window - 128 :] = edge.astype(bf)
            if window > 128:
                out_ref[k, :, : window - 128] = rows_ref[:, at:last]


def share_windows(rows, fold, hidden, width, reps):
    share = width // reps
    window = share + 64
    starts = tuple((k * share // 128 * 128, k * share % 128 != 0) for k in range(reps))
    vmem = pl.BlockSpec(memory_space=pltpu.VMEM)
    return pl.pallas_call(
        functools.partial(window_kernel, hidden, width, starts),
        out_shape=jax.ShapeDtypeStruct((reps, rows.shape[0], window), jnp.bfloat16),
        in_specs=[vmem, vmem],
        out_specs=vmem,
        compiler_params=pltpu.CompilerParams(vmem_limit_bytes=16 * 1024 * 1024),
        cost_estimate=pl.CostEstimate(flops=0, bytes_accessed=1024, transcendentals=0),
    )(rows, fold)


def on_device(activations, cotangent, gates, experts, groups, weights):
    reps = lax.axis_size("rep")
    nodes = lax.axis_size("node")
    xs = lax.axis_size("x")
    locals_ = xs * lax.axis_size("half")
    tokens, width = activations.shape
    hidden = weights.shape[2]
    slots = experts.shape[1]
    named = groups.shape[1]
    per_group = slots // named
    block = nodes // named
    blocks = tokens // block
    rows_one = nodes * blocks
    cap = max(rows_one // 3, (per_group * rows_one + locals_ - 1) // locals_)
    total = nodes * locals_
    bf = jnp.bfloat16
    f32 = jnp.float32
    pairs = partner_pairs(reps)
    rep_at = lax.axis_index("rep")
    node_at = lax.axis_index("node")
    x_at = lax.axis_index("x")
    half_at = lax.axis_index("half")

    expert_full = jnp.repeat(groups, per_group, axis=1) * locals_ + experts
    gate_wide = jnp.sum(
        jnp.where(
            expert_full[:, :, None] == jnp.arange(total, dtype=jnp.int32)[None, None, :],
            gates.astype(f32)[:, :, None],
            0.0,
        ),
        axis=1,
    ).astype(bf)
    own = jnp.concatenate([cotangent, activations, gate_wide], axis=1)
    wide = own.shape[1]
    other = lax.ppermute(own, ("rep", "half"), pairs)
    both = jnp.concatenate([own, other], axis=0)

    places = 2 * rows_one
    place_index = jnp.arange(places, dtype=jnp.int32)
    place_expert = (
        (place_index // (2 * blocks))[:, None]
        == (jnp.arange(total, dtype=jnp.int32) // locals_)[None, :]
    ).astype(bf)
    named_both = (both[:, width + hidden :] != 0).astype(bf)
    hit = lax.dot_general(
        place_expert, named_both, (((1,), (1,)), ((), ())), preferred_element_type=f32
    )
    placing = (
        (hit > 0)
        & (
            (place_index % (2 * blocks))[:, None]
            == (jnp.arange(2 * tokens, dtype=jnp.int32) // block)[None, :]
        )
    ).astype(bf)
    send_rows = jnp.dot(placing, both, preferred_element_type=f32).astype(bf)
    rows = lax.all_to_all(
        send_rows.reshape(nodes, 2 * blocks, wide), "node", 0, 0, tiled=True
    ).reshape(places, wide)

    filled = 2 * cap
    cap2 = -(-filled // 16) * 16
    before = (place_index[:, None] < place_index[None, :]).astype(bf)
    slot_at = jnp.arange(cap2, dtype=jnp.int32).astype(f32)

    def pickers(gates_here):
        named_here = (gates_here != 0).astype(f32)
        result = []
        for j in range(xs):
            mine_local = jnp.arange(locals_) == (x_at + j) % xs * 2 + half_at
            live = jnp.sum(jnp.where(mine_local[:, None], named_here, 0.0), axis=-2)
            rank = jnp.dot(live.astype(bf), before, preferred_element_type=f32)
            result.append(
                ((live[..., None, :] > 0) & (rank[..., None, :] == slot_at[:, None])).astype(bf)
            )
        return result

    share = width // reps
    group_expert = (
        (node_at * locals_ + jnp.arange(locals_, dtype=jnp.int32))[:, None]
        == jnp.arange(total, dtype=jnp.int32)[None, :]
    ).astype(bf)
    group_gates = lax.dot_general(
        group_expert,
        rows[:, width + hidden :],
        (((1,), (1,)), ((), ())),
        preferred_element_type=f32,
    ).astype(bf)
    window = share + 64
    offset = rep_at * share % 128
    gate_start = jnp.where(offset == 0, share, 0)
    lane = jnp.arange(window, dtype=jnp.int32)
    narrow = jnp.arange(128, dtype=jnp.int32)
    fold = (
        (jnp.arange(total, dtype=jnp.int32)[:, None] == (node_at * locals_ + narrow % 64)[None, :])
        & (narrow % 64 < locals_)[None, :]
    ).astype(bf)
    cols = share_windows(rows, fold, hidden, width, reps)
    cols = lax.all_to_all(cols, "rep", 0, 0, tiled=True)

    picker = pickers(group_gates)
    sent = [
        jnp.dot(p, rows, preferred_element_type=f32).astype(bf) for p in picker[1:]
    ]
    moved = [lax.ppermute(sent[j - 1], "x", ring(xs, j)) for j in range(1, xs)]
    slabs = [jnp.dot(picker[0], rows, preferred_element_type=f32).astype(bf)] + moved

    mine = jnp.arange(total, dtype=jnp.int32) == node_at * locals_ + x_at * 2 + half_at
    back, grad_pre = expert(slabs, weights, mine.astype(f32)[None, :])

    gathered = lax.all_gather(grad_pre, "rep", axis=0, tiled=True)

    back_slots = jnp.concatenate(
        [back[0]]
        + [
            lax.ppermute(back[j], "x", ring(xs, -j))
            for j in range(1, xs)
        ],
        axis=0,
    )
    back_rows = lax.dot_general(
        jnp.concatenate(picker, axis=0),
        back_slots,
        (((0,), (0,)), ((), ())),
        preferred_element_type=f32,
    ).astype(bf)
    back_rows, cols = lax.optimization_barrier((back_rows, cols))
    home_rows = lax.all_to_all(
        back_rows.reshape(nodes, 2 * blocks, wide), "node", 0, 0, tiled=True
    ).reshape(places, wide)

    gate_lane = (
        gate_start + jnp.arange(locals_, dtype=jnp.int32)[:, None] == lane[None, :]
    ).astype(bf)
    all_gates = jnp.einsum("lc,prc->plr", gate_lane, cols, preferred_element_type=f32)
    share_sent = [
        jnp.einsum("pcr,prd->pcd", p, cols, preferred_element_type=f32).astype(bf)
        for p in pickers(all_gates)
    ]
    share_rows = [share_sent[0]] + [
        lax.ppermute(share_sent[j], "x", ring(xs, j)) for j in range(1, xs)
    ]
    x_cols = jnp.stack(share_rows, axis=1)
    x_cols = lax.dynamic_slice_in_dim(
        x_cols.reshape(reps * xs * cap2, window), offset, share, 1
    )
    grad_share = lax.dot_general(
        x_cols, gathered, (((0,), (0,)), ((), ())), preferred_element_type=f32
    )
    home = lax.dot_general(
        placing, home_rows, (((0,), (0,)), ((), ())), preferred_element_type=f32
    )
    returned = lax.ppermute(home[tokens:].astype(bf), ("rep", "half"), pairs)
    returned, grad_share = lax.optimization_barrier((returned, grad_share))
    result = home[:tokens] + returned.astype(f32)
    grad_activations = result[:, hidden : hidden + width].astype(bf)
    output = result[:, :hidden].astype(bf)
    gate_back = result[:, width + hidden :]
    grad_gates = jnp.sum(
        jnp.where(
            expert_full[:, :, None] == jnp.arange(total, dtype=jnp.int32)[None, None, :],
            gate_back[:, None, :],
            0.0,
        ),
        axis=2,
    ).astype(bf)
    return (output, grad_activations, grad_gates, grad_share[None])


def solution(mesh):
    reps, nodes, locals_ = (mesh.shape[name] for name in ("rep", "node", "local"))
    fine = Mesh(mesh.devices.reshape(reps, nodes, locals_ // 2, 2), ALL)
    rows = P(ALL, None)
    return jax.shard_map(
        on_device,
        mesh=fine,
        in_specs=(rows, rows, rows, rows, rows, P(("node", "x", "half"), None, None)),
        out_specs=(rows, rows, rows, P(("node", "x", "half"), "rep", None)),
        check_vma=False,
    )
```
